32 devices in a mesh: col: 8 (over z, x), row: 4 (over y, core).
Axes of the slice: x: 2, y: 2, z: 4, core: 2. Of those that a mesh axis runs over, the one named last changes fastest.
Arguments:
- amplitudes: bfloat16 [512, 16384], P(None, ('col', 'row')), may hold values from -6 to 6
- integrals: bfloat16 [4096, 8192], P('row', 'col'), may hold values from -0.09375 to 0.09375
- wanted: int32 [8, 4, 8], replicated, may hold values from 0 to 31, as said below
- owner: int32 [64], replicated, may hold values from 0 to 63, each once
Outputs:
- ladder: bfloat16 [512, 8192], P(('col', 'row'))
The draws below stay inside these ranges and needn't reach their ends.
Inputs may be any that keep to these rules, and one draw needn't show every extreme that they name: Each list wanted[c, r, :] names 8 distinct values; at most 2 of them share one value of w // 4, and every list has 2 for at least one such value. `owner`: A permutation of the result tiles.
All inputs are finite; a program needn't handle non-finite values.
Results may differ from the reference program's by a relative error of at most 0.001.
Values may be sent and summed in bfloat16 or wider, within the bound.
No kernel may reach another device: no remote copies, remote signals or barrier semaphores. Data moves between devices by JAX's collectives and lax.ppermute only.
A program may use at most 128 MiB of HBM per device.

```python
import jax
import jax.numpy as jnp
from jax import lax

TILE = 128
NPAIR = 512
SRC_T = 4
CAP = 2
CT = 8
KL = 8
KT = 128
NABT = 64
N_COL = 8
N_ROW = 4


def one_list(key):
    key_full, key_order, key_inner, key_score = jax.random.split(key, 4)
    lowest = max(1, -(-(KL - N_COL) // (CAP - 1)))
    highest = KL // CAP
    full_count = jax.random.randint(key_full, (), lowest, highest + 1)
    single_count = KL - full_count * CAP
    sequence = jax.random.permutation(key_order, N_COL)
    position = jnp.argsort(sequence)
    counts = jnp.where(position < full_count, CAP, jnp.where(position < full_count + single_count, 1, 0))
    inner_keys = jax.random.split(key_inner, N_COL)
    inner_rank = jax.vmap(tile_rank)(inner_keys)
    keeping = inner_rank < counts[:, None]
    scores = jax.random.permutation(key_score, N_COL * SRC_T)
    sort_keys = jnp.where(keeping.reshape(-1), scores, scores + N_COL * SRC_T)
    picked = jnp.argsort(sort_keys)[:KL]
    return picked.astype(jnp.int32)


def tile_rank(key):
    return jnp.argsort(jax.random.permutation(key, SRC_T))


def draw_wanted(key, part):
    key = jax.random.fold_in(key, 11)
    list_keys = jax.random.split(key, N_COL * N_ROW)
    lists = jax.vmap(one_list)(list_keys)
    return lists.reshape(N_COL, N_ROW, KL)


def block_levels(key, dims, pieces, least, largest):
    gain, own = 1.0, jax.random.fold_in(key, 6)
    for dim, shards_of in pieces:
        steps = jnp.exp(jax.random.uniform(jax.random.fold_in(own, dim), (shards_of,), jnp.float32, least / len(pieces), largest / len(pieces)))
        gain = gain * jnp.repeat(steps, dims[dim] // shards_of).reshape([-1 if axis == dim else 1 for axis in range(len(dims))])
    return gain


def bell_draw(rng, dims, deviation, most, shards=(), held_as=jnp.bfloat16):
    factor_of = block_levels(rng, dims, shards, -0.22, 0.18) if shards else 1.0
    drawn = jax.random.normal(rng, dims, jnp.float32) * deviation * factor_of
    return jnp.minimum(jnp.maximum(drawn, -most), most).astype(held_as)


def setup_inputs(seed: int = 0) -> dict:
    key_list = jax.random.split(jax.random.key(seed), 5)
    amplitudes = bell_draw(key_list[0], (NPAIR, KT * TILE), 1.0, 6.0, ((1, 32),))
    integrals = bell_draw(key_list[1], (N_ROW * KL * TILE, N_COL * CT * TILE), (N_ROW * KL * TILE) ** -0.5, 0.09375, ((0, 4), (1, 8)))
    wanted = draw_wanted(jax.random.fold_in(key_list[4], 71), 0)
    owner = jax.random.permutation(key_list[3], NABT).astype(jnp.int32)
    return {"amplitudes": amplitudes, "integrals": integrals, "wanted": wanted, "owner": owner}


def reference(amplitudes, integrals, wanted, owner):
    tile_view = amplitudes.reshape(NPAIR, KT, TILE)
    row_ids = jnp.arange(N_ROW, dtype=jnp.int32)

    def one_column(column):
        listed = wanted[column]
        global_ids = ((listed // SRC_T) * N_ROW + row_ids[:, None]) * SRC_T + listed % SRC_T
        selected = jnp.take(tile_view, global_ids.reshape(-1), axis=1).reshape(NPAIR, N_ROW * KL * TILE)
        column_block = lax.dynamic_slice_in_dim(integrals, (column * (CT * TILE)).astype(jnp.int32), CT * TILE, 1)
        return jnp.dot(selected, column_block, preferred_element_type=jnp.float32).astype(jnp.bfloat16)

    held_tiles = lax.map(one_column, jnp.arange(N_COL, dtype=jnp.int32))
    held_tiles = held_tiles.reshape(N_COL, NPAIR, CT, TILE)
    source_dev = owner // CT
    slot_ids = owner % CT
    ordered = held_tiles[source_dev, :, slot_ids, :]
    return jnp.transpose(ordered, (1, 0, 2)).reshape(NPAIR, NABT * TILE)
```

```python
import functools

import jax
import jax.numpy as jnp
from jax import lax
from jax.experimental import pallas as pl
from jax.experimental.pallas import tpu as pltpu
from jax.sharding import PartitionSpec as P

TILE = 128
CAP = 2
ANY = pl.BlockSpec(memory_space=pl.ANY)
SMEM = pl.BlockSpec(memory_space=pltpu.SMEM)
VMEM = pl.BlockSpec(memory_space=pltpu.VMEM)
LIMIT = 48 * 1024 * 1024


def halving_order(count):
    bits = count.bit_length() - 1
    return [int(format(count - 1 - j, "b").zfill(bits)[::-1], 2) for j in range(count)]


def select_kernel(per_source, wanted, amps, *rest):
    outs, sem = rest[:-1], rest[-1]
    me, row = lax.axis_index("col"), lax.axis_index("row")
    length = wanted.shape[2]
    copies = []
    for d in range(1, len(outs) + 1):
        other = me ^ d

        def step(k, found):
            first, second, count = found
            w = wanted[other, row, k]
            mine = w // per_source == me
            tile = w % per_source
            first = jnp.where(mine & (count == 0), tile, first)
            second = jnp.where(mine & (count == 1), tile, second)
            return first, second, count + mine.astype(jnp.int32)

        zero = jnp.int32(0)
        found = lax.fori_loop(0, length, step, (zero, zero, zero), unroll=length <= 8)
        for slot in range(CAP):
            start = pl.multiple_of(found[slot] * TILE, TILE)
            copy = pltpu.make_async_copy(amps.at[:, pl.ds(start, TILE)], outs[d - 1].at[slot], sem.at[d - 1, slot])
            copy.start()
            copies.append(copy)
    for copy in copies:
        copy.wait()


def select(wanted, amps, per_source, count):
    shape = jax.ShapeDtypeStruct((CAP, amps.shape[0], TILE), amps.dtype)
    return pl.pallas_call(
        functools.partial(select_kernel, per_source),
        out_shape=[shape] * count,
        in_specs=[SMEM, VMEM],
        out_specs=[ANY] * count,
        scratch_shapes=[pltpu.SemaphoreType.DMA((count, CAP))],
        compiler_params=pltpu.CompilerParams(vmem_limit_bytes=LIMIT),
        name="select_tiles",
    )(wanted, amps)


def contract_kernel(per_source, sources, wanted, own, *rest):
    received = rest[:sources - 1]
    block, send, keep, left, right, result, sem_left, sem_right, sem_out = rest[sources - 1:]
    me, row = lax.axis_index("col"), lax.axis_index("row")
    length = wanted.shape[2]
    parts = left.shape[0]
    order = halving_order(parts)
    load_block = pltpu.make_async_copy(block, right, sem_right)
    load_block.start()

    def fetch(k, carry):
        w = wanted[me, row, k]
        source = w // per_source
        slot = lax.fori_loop(0, k, lambda i, n: n + (wanted[me, row, i] // per_source == source).astype(jnp.int32), jnp.int32(0))
        away = source ^ me
        columns = pl.ds(pl.multiple_of(k * TILE, TILE), TILE)
        own_columns = pl.ds(pl.multiple_of((w % per_source) * TILE, TILE), TILE)

        @pl.when(away == 0)
        def _():
            for j in range(parts):
                pltpu.make_async_copy(own.at[:, row ^ order[j], :, own_columns], left.at[j, :, :, columns], sem_left).start()

        for d in range(1, sources):
            @pl.when(away == d)
            def _():
                for j in range(parts):
                    pltpu.make_async_copy(received[d - 1].at[slot, :, row ^ order[j]], left.at[j, :, :, columns], sem_left).start()
        return carry

    lax.fori_loop(0, length, fetch, 0)
    load_block.wait()
    pltpu.make_async_copy(left, left, sem_left).wait()
    half = parts // 2
    rows = result.shape[1]
    depth = left.shape[3]
    outs = []
    for h, target in ((0, send), (1, keep)):
        a = left[h * half:(h + 1) * half].reshape(rows, depth)
        result[h] = jnp.dot(a, right[...], preferred_element_type=jnp.float32)
        copy = pltpu.make_async_copy(result.at[h], target, sem_out.at[h])
        copy.start()
        outs.append(copy)
    for copy in outs:
        copy.wait()


def contract(wanted, own, received, block, per_source):
    a, parts, b, _ = own.shape
    depth, width = block.shape
    rows = a * parts * b // 2
    shape = jax.ShapeDtypeStruct((rows, width), jnp.float32)
    return pl.pallas_call(
        functools.partial(contract_kernel, per_source, len(received) + 1),
        out_shape=[shape, shape],
        in_specs=[SMEM] + [ANY] * (len(received) + 2),
        out_specs=[ANY, ANY],
        scratch_shapes=[
            pltpu.VMEM((parts, a, b, depth), own.dtype),
            pltpu.VMEM((depth, width), block.dtype),
            pltpu.VMEM((2, rows, width), jnp.float32),
            pltpu.SemaphoreType.DMA,
            pltpu.SemaphoreType.DMA,
            pltpu.SemaphoreType.DMA((2,)),
        ],
        compiler_params=pltpu.CompilerParams(vmem_limit_bytes=LIMIT),
        name="contract_tiles",
    )(wanted, own, *received, block)


def reorder_kernel(tiles_held, owner, received, out):
    for t in range(owner.shape[0]):
        at = owner[t]
        start = pl.multiple_of((at % tiles_held) * TILE, TILE)
        out[:, t * TILE:(t + 1) * TILE] = received[at // tiles_held, :, pl.ds(start, TILE)]


def reorder(owner, received):
    columns, rows, width = received.shape
    return pl.pallas_call(
        functools.partial(reorder_kernel, width // TILE),
        out_shape=jax.ShapeDtypeStruct((rows, columns * width), received.dtype),
        in_specs=[SMEM, VMEM],
        out_specs=VMEM,
        compiler_params=pltpu.CompilerParams(vmem_limit_bytes=LIMIT),
        name="reorder_tiles",
    )(owner, received)


def body(amplitudes, integrals, wanted, owner):
    columns = lax.axis_size("col")
    parts = lax.axis_size("row")
    pairs = amplitudes.shape[0]
    per_source = amplitudes.shape[1] // TILE
    per_device = pairs // (columns * parts)
    if per_device % 16 == 0:
        rows_view = (columns, parts, per_device)
    else:
        amplitudes = amplitudes.reshape(columns, parts, per_device, -1).transpose(1, 0, 2, 3).reshape(pairs, -1)
        rows_view = (1, parts, columns * per_device)
    parcels = select(wanted, amplitudes, per_source, columns - 1)
    received = []
    for d in range(1, columns):
        moved = lax.ppermute(parcels[d - 1], "col", [(c, c ^ d) for c in range(columns)])
        received.append(moved.reshape((CAP,) + rows_view + (TILE,)))
    send, keep = contract(wanted, amplitudes.reshape(rows_view + (-1,)), received, integrals, per_source)
    bit = 1
    while True:
        arrived = lax.ppermute(send, "row", [(r, r ^ bit) for r in range(parts)])
        bit *= 2
        if bit == parts:
            break
        half = keep.shape[0] // 2
        send = keep[:half] + arrived[:half]
        keep = keep[half:] + arrived[half:]
    held = (keep + arrived).astype(jnp.bfloat16)
    held = held.reshape(columns, per_device, -1)
    exchanged = lax.all_to_all(held, "col", split_axis=0, concat_axis=0, tiled=True)
    return reorder(owner, exchanged)


def solution(mesh):
    in_specs = (P(None, ("col", "row")), P("row", "col"), P(), P())
    out_specs = P(("col", "row"), None)
    return jax.shard_map(body, mesh=mesh, in_specs=in_specs, out_specs=out_specs, check_vma=False)
```

```python
import functools

import jax
import jax.numpy as jnp
from jax import lax
from jax.experimental import pallas as pl
from jax.experimental.pallas import tpu as pltpu
from jax.sharding import PartitionSpec as P

TILE = 128
CAP = 2
CORES = 2
SMALL = 8 * 1024 * 1024
LEAST = 2.0 ** -125
STEPS = 32766.0
ANY = pl.BlockSpec(memory_space=pl.ANY)
SMEM = pl.BlockSpec(memory_space=pltpu.SMEM)
VMEM = pl.BlockSpec(memory_space=pltpu.VMEM)


def params(size=0):
    return pltpu.CompilerParams(vmem_limit_bytes=size + SMALL)


def halving_order(count):
    bits = count.bit_length() - 1
    return [int(format(count - 1 - j, "b").zfill(bits)[::-1], 2) for j in range(count)] if bits else [0]


def split_kernel(amps, mine, theirs, sem):
    core = lax.axis_index("row") % CORES
    copies = [
        pltpu.make_async_copy(amps.at[:, :, core], mine, sem.at[0]),
        pltpu.make_async_copy(amps.at[:, :, 1 - core], theirs, sem.at[1]),
    ]
    for copy in copies:
        copy.start()
    for copy in copies:
        copy.wait()


def split(amps):
    shape = jax.ShapeDtypeStruct(amps.shape[:2] + amps.shape[3:], amps.dtype)
    return pl.pallas_call(
        split_kernel,
        out_shape=[shape, shape],
        in_specs=[ANY],
        out_specs=[ANY, ANY],
        scratch_shapes=[pltpu.SemaphoreType.DMA((2,))],
        compiler_params=params(),
        name="split_rows",
    )(amps)


def select_kernel(per_source, away, flips, wanted, *rest):
    groups, outs, sem = rest[:CORES], rest[CORES:-1], rest[-1]
    me, row = lax.axis_index("col"), lax.axis_index("row")
    length = wanted.shape[2]
    source = me ^ away
    copies = []
    for n, flip in enumerate(flips):
        other = me ^ flip
        for g in range(CORES):

            def step(k, found):
                first, second, count = found
                w = wanted[other, row ^ g, k]
                mine = w // per_source == source
                tile = w % per_source
                first = jnp.where(mine & (count == 0), tile, first)
                second = jnp.where(mine & (count == 1), tile, second)
                return first, second, count + mine.astype(jnp.int32)

            zero = jnp.int32(0)
            found = lax.fori_loop(0, length, step, (zero, zero, zero), unroll=length <= 8)
            for slot in range(CAP):
                start = pl.multiple_of(found[slot] * TILE, TILE)
                copy = pltpu.make_async_copy(groups[g].at[:, pl.ds(start, TILE)], outs[n].at[g, slot], sem.at[n, g, slot])
                copy.start()
                copies.append(copy)
    for copy in copies:
        copy.wait()


def select(wanted, groups, per_source, away, flips):
    rows = groups[0].shape[0]
    shape = jax.ShapeDtypeStruct((CORES, CAP, rows, TILE), groups[0].dtype)
    return pl.pallas_call(
        functools.partial(select_kernel, per_source, away, flips),
        out_shape=[shape] * len(flips),
        in_specs=[SMEM] + [ANY] * CORES,
        out_specs=[ANY] * len(flips),
        scratch_shapes=[pltpu.SemaphoreType.DMA((len(flips), CORES, CAP))],
        compiler_params=params(),
        name="select_tiles",
    )(wanted, *groups)


def arrange_kernel(per_source, top, wanted, *refs):
    blocks, (early, far) = refs[:CORES], refs[CORES:]
    me, row = lax.axis_index("col"), lax.axis_index("row")
    length = wanted.shape[2]
    for part in (early, far):
        part[...] = jnp.zeros_like(part)
    near_base = CORES * per_source
    whole_base = near_base + CORES * CAP * (top - 1)
    for g in range(CORES):

        def place(k, carry):
            w = wanted[me, row ^ g, k]
            source = w // per_source
            slot = lax.fori_loop(0, k, lambda i, n: n + (wanted[me, row ^ g, i] // per_source == source).astype(jnp.int32), jnp.int32(0))
            away, tile = source ^ me, w % per_source
            passed = CAP * (CORES * (lax.rem(away, top) - 1) + g) + slot
            rows = blocks[g][pl.ds(pl.multiple_of(k * TILE, TILE), TILE)]

            def put(part, condition, at):
                @pl.when(condition)
                def _():
                    part[pl.ds(pl.multiple_of(at * TILE, TILE), TILE)] = rows

            put(early, away == 0, g * per_source + tile)
            put(early, (away > 0) & (away < top), near_base + passed)
            put(early, away == top, whole_base + g * per_source + tile)
            put(far, away > top, passed)
            return carry

        lax.fori_loop(0, length, place, 0)


def arrange(wanted, blocks, per_source, top):
    depth, width = blocks[0].shape
    passed = CORES * CAP * (top - 1)
    depths = [TILE * n for n in (2 * CORES * per_source + passed, passed)]
    part = width if depth <= 1024 else width // 4
    size = 4 * part * (CORES * depth + sum(depths))
    return pl.pallas_call(
        functools.partial(arrange_kernel, per_source, top),
        grid=(width // part,),
        out_shape=[jax.ShapeDtypeStruct((n, width), blocks[0].dtype) for n in depths],
        in_specs=[SMEM] + [pl.BlockSpec((depth, part), lambda n: (0, n))] * CORES,
        out_specs=[pl.BlockSpec((n, part), lambda n: (0, n)) for n in depths],
        compiler_params=params(size),
        name="arrange_block",
    )(wanted, *blocks)


def code(x):
    most = jnp.max(jnp.abs(x), axis=1, keepdims=True)
    power = jnp.clip(jnp.ceil(jnp.log2(jnp.maximum(most, LEAST))), -125.0, 120.0)
    scaled = jnp.floor(x * jnp.exp2(-power) * STEPS + 0.5)
    scaled = jnp.clip(scaled, -32767.0, 32767.0).astype(jnp.int32).astype(jnp.int16)
    powers = jnp.broadcast_to(power, (x.shape[0], TILE)).astype(jnp.int32).astype(jnp.int16)
    return scaled, powers


def decode(coded):
    width = coded.shape[1] - TILE
    power = coded[:, width:].astype(jnp.int32).astype(jnp.float32)[:, :1]
    return coded[:, :width].astype(jnp.int32).astype(jnp.float32) * (1 / STEPS) * jnp.exp2(power)


def steps(rows):
    size = 64 if rows % 64 == 0 else 32 if rows % 32 == 0 else 16
    return [slice(start, start + size) for start in range(0, rows, size)]


def put_coded(out, at, x):
    width = x.shape[1]
    out[at, :width], out[at, width:] = code(x)


def fill(left, source, flip, depth, at):
    y = (lax.axis_index("row") // CORES) ^ flip
    rows = pl.ds(at, source.shape[-4] * source.shape[-2])
    if len(source.shape) == 4:
        tiles = [source[:, y]]
    else:
        tiles = [source[g, slot, :, y] for g in range(CORES) for slot in range(CAP)]
    for tile in tiles:
        width = tile.shape[-1]
        left[rows, depth:depth + width] = tile.reshape(-1, width)
        depth += width
    return depth


def contract_kernel(count, slots, coded, *refs):
    sources, block = refs[:count], refs[count]
    before, outs, left = refs[count + 1:-1 - len(slots)], refs[-1 - len(slots):-1], refs[-1]
    for n, flips in enumerate(slots):
        for j, flip in enumerate(flips):
            depth = 0
            for source in sources:
                depth = fill(left, source, flip, depth, j * (left.shape[0] // len(flips)))
        x = jnp.dot(left[...], block[...], preferred_element_type=jnp.float32)
        if before:
            x = before[n][...] + x
        if coded:
            put_coded(outs[n], slice(None), x)
        else:
            outs[n][...] = x


def contract(sources, block, slots, before=(), coded=False):
    depth, width = block.shape
    rows = sources[0].shape[-4] * sources[0].shape[-2] * len(slots[0])
    if coded:
        shape = jax.ShapeDtypeStruct((rows, width + TILE), jnp.int16)
    else:
        shape = jax.ShapeDtypeStruct((rows, width), jnp.float32)
    size = 2 * depth * (width + rows) + 12 * width * rows * len(slots) + sum(2 * x.size for x in sources)
    return pl.pallas_call(
        functools.partial(contract_kernel, len(sources), slots, coded),
        out_shape=[shape] * len(slots),
        in_specs=[VMEM] * (len(sources) + 1 + len(before)),
        out_specs=[VMEM] * len(slots),
        scratch_shapes=[pltpu.VMEM((rows, depth), block.dtype)],
        compiler_params=params(size),
        name="contract_tiles",
    )(*sources, block, *before)


def fold_kernel(keep, arrived, send, kept):
    half = kept.shape[0]
    for at in steps(half):
        put_coded(send, at, keep[at] + decode(arrived[at]))
    for at in steps(half):
        low = slice(at.start + half, at.stop + half)
        kept[at] = keep[low] + decode(arrived[low])


def fold(keep, arrived):
    half, width = keep.shape[0] // 2, keep.shape[1]
    return pl.pallas_call(
        fold_kernel,
        out_shape=[jax.ShapeDtypeStruct((half, width + TILE), jnp.int16), jax.ShapeDtypeStruct((half, width), jnp.float32)],
        in_specs=[VMEM, VMEM],
        out_specs=[VMEM, VMEM],
        compiler_params=params(),
        name="fold_rows",
    )(keep, arrived)


def finish_kernel(keep, arrived, out):
    for at in steps(keep.shape[0]):
        out[at] = (keep[at] + decode(arrived[at])).astype(out.dtype)


def finish(keep, arrived):
    return pl.pallas_call(
        finish_kernel,
        out_shape=jax.ShapeDtypeStruct(keep.shape, jnp.bfloat16),
        in_specs=[VMEM, VMEM],
        out_specs=VMEM,
        compiler_params=params(),
        name="finish_rows",
    )(keep, arrived)


def reorder_kernel(tiles_held, owner, received, out):
    for t in range(owner.shape[0]):
        at = owner[t]
        start = pl.multiple_of((at % tiles_held) * TILE, TILE)
        out[:, t * TILE:(t + 1) * TILE] = received[at // tiles_held, :, pl.ds(start, TILE)]


def reorder(owner, received):
    columns, rows, width = received.shape
    return pl.pallas_call(
        functools.partial(reorder_kernel, width // TILE),
        out_shape=jax.ShapeDtypeStruct((rows, columns * width), received.dtype),
        in_specs=[SMEM, VMEM],
        out_specs=VMEM,
        compiler_params=params(),
        name="reorder_tiles",
    )(owner, received)


def swap(x, axis, flip):
    return lax.ppermute(x, axis, [(i, i ^ flip) for i in range(lax.axis_size(axis))])


def body(amplitudes, integrals, wanted, owner):
    columns = lax.axis_size("col")
    parts = lax.axis_size("row")
    ys = parts // CORES
    pairs = amplitudes.shape[0]
    per_source = amplitudes.shape[1] // TILE
    per_device = pairs // (columns * parts)
    top = columns // 2
    low = list(range(1, top))
    b = max(per_device, 16)
    units = pairs // (parts * b)
    if b != per_device:
        amplitudes = amplitudes.reshape(units, columns // units, parts, per_device, -1).transpose(0, 2, 1, 3, 4)
    order = halving_order(ys)
    slots = [order[:ys // 2], order[ys // 2:]]

    def whole(x):
        return x.reshape(units, ys, b, -1)

    def near(groups, away):
        picked = select(wanted, [x.reshape(units * ys * b, -1) for x in groups], per_source, away, low)
        return [swap(x, "col", f).reshape(CORES, CAP, units, ys, b, TILE) for x, f in zip(picked, low)]

    mine, theirs = split(amplitudes.reshape(units, ys, CORES, b, -1))
    own = [mine, swap(theirs, "row", 1)]
    mirrors = [whole(swap(x, "col", top)) for x in own]
    nearby = near(own, 0)
    blocks = arrange(wanted, [integrals, swap(integrals, "row", 1)], per_source, top)
    *mirrors, early_block, far_block = lax.optimization_barrier((*mirrors, *blocks))
    far = near(mirrors, top)
    sums = contract(own + nearby + mirrors, early_block, slots)
    send, = contract(far, far_block, slots[:1], sums[:1], coded=True)
    keep, = contract(far, far_block, slots[1:], sums[1:])
    bit = CORES
    while True:
        arrived = swap(send, "row", bit)
        bit *= 2
        if bit == parts:
            break
        send, keep = fold(keep, arrived)
    held = finish(keep, arrived).reshape(columns, per_device, -1)
    exchanged = lax.all_to_all(held, "col", split_axis=0, concat_axis=0, tiled=True)
    return reorder(owner, exchanged)


def solution(mesh):
    in_specs = (P(None, ("col", "row")), P("row", "col"), P(), P())
    out_specs = P(("col", "row"), None)
    return jax.shard_map(body, mesh=mesh, in_specs=in_specs, out_specs=out_specs, check_vma=False)
```

```python
import functools

import jax
import jax.numpy as jnp
from jax import lax
from jax.experimental import pallas as pl
from jax.experimental.pallas import tpu as pltpu
from jax.sharding import PartitionSpec as P

TILE = 128
CAP = 2
CORES = 2
FIRST = 2
SMALL = 8 * 1024 * 1024
LEAST = 2.0 ** -125
STEPS = 32766.0
ANY = pl.BlockSpec(memory_space=pl.ANY)
SMEM = pl.BlockSpec(memory_space=pltpu.SMEM)
VMEM = pl.BlockSpec(memory_space=pltpu.VMEM)


def params(size=0):
    return pltpu.CompilerParams(vmem_limit_bytes=size + SMALL)


def halving_order(count):
    bits = count.bit_length() - 1
    return [int(format(count - 1 - j, "b").zfill(bits)[::-1], 2) for j in range(count)] if bits else [0]


def split_kernel(amps, mine, theirs, sem):
    core = lax.axis_index("row") % CORES
    copies = [
        pltpu.make_async_copy(amps.at[:, :, core], mine, sem.at[0]),
        pltpu.make_async_copy(amps.at[:, :, 1 - core], theirs, sem.at[1]),
    ]
    for copy in copies:
        copy.start()
    for copy in copies:
        copy.wait()


def split(amps):
    shape = jax.ShapeDtypeStruct(amps.shape[:2] + amps.shape[3:], amps.dtype)
    return pl.pallas_call(
        split_kernel,
        out_shape=[shape, shape],
        in_specs=[ANY],
        out_specs=[ANY, ANY],
        scratch_shapes=[pltpu.SemaphoreType.DMA((2,))],
        compiler_params=params(),
        name="split_rows",
    )(amps)


def select_kernel(per_source, away, flips, wanted, *rest):
    groups, outs, sem = rest[:CORES], rest[CORES:-1], rest[-1]
    me, row = lax.axis_index("col"), lax.axis_index("row")
    length = wanted.shape[2]
    source = me ^ away
    copies = []
    for n, flip in enumerate(flips):
        other = me ^ flip
        for g in range(CORES):

            def step(k, found):
                first, second, count = found
                w = wanted[other, row ^ g, k]
                mine = w // per_source == source
                tile = w % per_source
                first = jnp.where(mine & (count == 0), tile, first)
                second = jnp.where(mine & (count == 1), tile, second)
                return first, second, count + mine.astype(jnp.int32)

            zero = jnp.int32(0)
            found = lax.fori_loop(0, length, step, (zero, zero, zero), unroll=length <= 8)
            for slot in range(CAP):
                start = pl.multiple_of(found[slot] * TILE, TILE)
                copy = pltpu.make_async_copy(groups[g].at[:, pl.ds(start, TILE)], outs[n].at[g, slot], sem.at[n, g, slot])
                copy.start()
                copies.append(copy)
    for copy in copies:
        copy.wait()


def select(wanted, groups, per_source, away, flips):
    rows = groups[0].shape[0]
    shape = jax.ShapeDtypeStruct((CORES, CAP, rows, TILE), groups[0].dtype)
    return pl.pallas_call(
        functools.partial(select_kernel, per_source, away, flips),
        out_shape=[shape] * len(flips),
        in_specs=[SMEM] + [ANY] * CORES,
        out_specs=[ANY] * len(flips),
        scratch_shapes=[pltpu.SemaphoreType.DMA((len(flips), CORES, CAP))],
        compiler_params=params(),
        name="select_tiles",
    )(wanted, *groups)


def choice_kernel(per_source, away, flips, wanted, *outs):
    me, row = lax.axis_index("col"), lax.axis_index("row")
    length = wanted.shape[2]
    source = me ^ away
    one = (lax.broadcasted_iota(jnp.int32, (TILE, TILE), 0) == lax.broadcasted_iota(jnp.int32, (TILE, TILE), 1)).astype(outs[0].dtype)
    for g, out in enumerate(outs):
        out[...] = jnp.zeros_like(out)
        for n, flip in enumerate(flips):
            other = me ^ flip

            def step(k, count):
                w = wanted[other, row ^ g, k]
                mine = w // per_source == source
                at = pl.ds(pl.multiple_of((w % per_source) * TILE, TILE), TILE)
                for slot in range(CAP):

                    @pl.when(mine & (count == slot))
                    def _():
                        low = (n * CAP + slot) * TILE
                        out[at, low:low + TILE] = one

                return count + mine.astype(jnp.int32)

            lax.fori_loop(0, length, step, jnp.int32(0))


def choice(wanted, per_source, away, flips, dtype):
    shape = jax.ShapeDtypeStruct((per_source * TILE, len(flips) * CAP * TILE), dtype)
    return pl.pallas_call(
        functools.partial(choice_kernel, per_source, away, flips),
        out_shape=[shape] * CORES,
        in_specs=[SMEM],
        out_specs=[VMEM] * CORES,
        compiler_params=params(4 * shape.size * CORES),
        name="choice_matrices",
    )(wanted)


def pass_on_kernel(ranges, *refs):
    groups, choices, outs = refs[:CORES], refs[CORES:2 * CORES], refs[2 * CORES:]
    count = len(outs) // len(ranges)
    for g in range(CORES):
        x = jnp.dot(groups[g][...], choices[g][...], preferred_element_type=jnp.float32).astype(outs[0].dtype)
        for m, (start, stop) in enumerate(ranges):
            for n in range(count):
                for slot in range(CAP):
                    low = (n * CAP + slot) * TILE
                    outs[m * count + n][g, slot] = x[start:stop, low:low + TILE]


def pass_on(groups, choices, ranges):
    rows, chosen = groups[0].shape[0], choices[0].shape[1]
    shapes = [jax.ShapeDtypeStruct((CORES, CAP, stop - start, TILE), groups[0].dtype) for start, stop in ranges for _ in range(chosen // (CAP * TILE))]
    size = sum(2 * x.size for x in (*groups, *choices)) + 4 * CORES * rows * chosen * 2
    return pl.pallas_call(
        functools.partial(pass_on_kernel, ranges),
        out_shape=shapes,
        in_specs=[VMEM] * (2 * CORES),
        out_specs=[VMEM] * len(shapes),
        compiler_params=params(size),
        name="pass_on_tiles",
    )(*groups, *choices)


def arrange_kernel(per_source, top, wanted, *refs):
    blocks, (early, far) = refs[:CORES], refs[CORES:]
    me, row = lax.axis_index("col"), lax.axis_index("row")
    length = wanted.shape[2]
    for part in (early, far):
        part[...] = jnp.zeros_like(part)
    near_base = CORES * per_source
    whole_base = near_base + CORES * CAP * (top - 1)
    for g in range(CORES):

        def place(k, carry):
            w = wanted[me, row ^ g, k]
            source = w // per_source
            slot = lax.fori_loop(0, k, lambda i, n: n + (wanted[me, row ^ g, i] // per_source == source).astype(jnp.int32), jnp.int32(0))
            away, tile = source ^ me, w % per_source
            passed = CAP * (CORES * (lax.rem(away, top) - 1) + g) + slot
            rows = blocks[g][pl.ds(pl.multiple_of(k * TILE, TILE), TILE)]

            def put(part, condition, at):
                @pl.when(condition)
                def _():
                    part[pl.ds(pl.multiple_of(at * TILE, TILE), TILE)] = rows

            put(early, away == 0, g * per_source + tile)
            put(early, (away > 0) & (away < top), near_base + passed)
            put(early, away == top, whole_base + g * per_source + tile)
            put(far, away > top, passed)
            return carry

        lax.fori_loop(0, length, place, 0)


def arrange(wanted, blocks, per_source, top):
    depth, width = blocks[0].shape
    passed = CORES * CAP * (top - 1)
    depths = [TILE * n for n in (2 * CORES * per_source + passed, passed)]
    part = width if depth <= 1024 else width // 4
    size = 4 * part * (CORES * depth + sum(depths))
    return pl.pallas_call(
        functools.partial(arrange_kernel, per_source, top),
        grid=(width // part,),
        out_shape=[jax.ShapeDtypeStruct((n, width), blocks[0].dtype) for n in depths],
        in_specs=[SMEM] + [pl.BlockSpec((depth, part), lambda n: (0, n))] * CORES,
        out_specs=[pl.BlockSpec((n, part), lambda n: (0, n)) for n in depths],
        compiler_params=params(size),
        name="arrange_block",
    )(wanted, *blocks)


def code(x):
    most = jnp.max(jnp.abs(x), axis=1, keepdims=True)
    power = jnp.clip(jnp.ceil(jnp.log2(jnp.maximum(most, LEAST))), -125.0, 120.0)
    scaled = jnp.floor(x * jnp.exp2(-power) * STEPS + 0.5)
    scaled = jnp.clip(scaled, -32767.0, 32767.0).astype(jnp.int32).astype(jnp.int16)
    powers = jnp.broadcast_to(power, (x.shape[0], TILE)).astype(jnp.int32).astype(jnp.int16)
    return scaled, powers


def decode(coded):
    width = coded.shape[1] - TILE
    power = coded[:, width:].astype(jnp.int32).astype(jnp.float32)[:, :1]
    return coded[:, :width].astype(jnp.int32).astype(jnp.float32) * (1 / STEPS) * jnp.exp2(power)


def steps(rows):
    size = 64 if rows % 64 == 0 else 32 if rows % 32 == 0 else 16
    return [slice(start, start + size) for start in range(0, rows, size)]


def put_coded(out, at, x):
    width = x.shape[1]
    out[at, :width], out[at, width:] = code(x)


def fill(left, source, units, flip, depth, at):
    y = (lax.axis_index("row") // CORES) ^ flip
    span = units[1] - units[0]
    low = units[0] if source.shape[-4] > span else 0
    rows = pl.ds(at, span * source.shape[-2])
    if len(source.shape) == 4:
        tiles = [source[low:low + span, y]]
    else:
        tiles = [source[g, slot, low:low + span, y] for g in range(source.shape[0]) for slot in range(CAP)]
    for tile in tiles:
        width = tile.shape[-1]
        left[rows, depth:depth + width] = tile.reshape(-1, width)
        depth += width
    return depth


def contract_kernel(count, pieces, coded, *refs):
    sources, block = refs[:count], refs[count]
    before, outs, left = refs[count + 1:-1 - len(pieces)], refs[-1 - len(pieces):-1], refs[-1]
    base = 0
    for n, (units, flips) in enumerate(pieces):
        rows = outs[n].shape[0] // len(flips)
        for j, flip in enumerate(flips):
            depth = 0
            for source in sources:
                depth = fill(left, source, units, flip, depth, base + j * rows)
        base += outs[n].shape[0]
    product = jnp.dot(left[...], block[...], preferred_element_type=jnp.float32)
    base = 0
    for n in range(len(pieces)):
        rows = outs[n].shape[0]
        x = product[base:base + rows]
        base += rows
        if before:
            x = before[n][...] + x
        if coded:
            put_coded(outs[n], slice(None), x)
        else:
            outs[n][...] = x


def contract(sources, block, pieces, before=(), coded=False):
    depth, width = block.shape
    rows = [(units[1] - units[0]) * sources[0].shape[-2] * len(flips) for units, flips in pieces]
    if coded:
        shapes = [jax.ShapeDtypeStruct((n, width + TILE), jnp.int16) for n in rows]
    else:
        shapes = [jax.ShapeDtypeStruct((n, width), jnp.float32) for n in rows]
    size = 2 * depth * (width + sum(rows)) + 16 * width * sum(rows) + sum(2 * x.size for x in sources)
    return pl.pallas_call(
        functools.partial(contract_kernel, len(sources), pieces, coded),
        out_shape=shapes,
        in_specs=[VMEM] * (len(sources) + 1 + len(before)),
        out_specs=[VMEM] * len(shapes),
        scratch_shapes=[pltpu.VMEM((sum(rows), depth), block.dtype)],
        compiler_params=params(size),
        name="contract_tiles",
    )(*sources, block, *before)


def fold_kernel(keep, arrived, send, kept):
    half = kept.shape[0]
    for at in steps(half):
        put_coded(send, at, keep[at] + decode(arrived[at]))
    for at in steps(half):
        low = slice(at.start + half, at.stop + half)
        kept[at] = keep[low] + decode(arrived[low])


def fold(keep, arrived):
    half, width = keep.shape[0] // 2, keep.shape[1]
    return pl.pallas_call(
        fold_kernel,
        out_shape=[jax.ShapeDtypeStruct((half, width + TILE), jnp.int16), jax.ShapeDtypeStruct((half, width), jnp.float32)],
        in_specs=[VMEM, VMEM],
        out_specs=[VMEM, VMEM],
        compiler_params=params(),
        name="fold_rows",
    )(keep, arrived)


def finish_kernel(*refs):
    out, base = refs[-1], 0
    for keep, arrived in zip(refs[:-1:2], refs[1:-1:2]):
        for at in steps(keep.shape[0]):
            out[base + at.start:base + at.stop] = (keep[at] + decode(arrived[at])).astype(out.dtype)
        base += keep.shape[0]


def finish(pieces):
    flat = [x for piece in pieces for x in piece]
    rows = sum(keep.shape[0] for keep, _ in pieces)
    return pl.pallas_call(
        finish_kernel,
        out_shape=jax.ShapeDtypeStruct((rows, flat[0].shape[1]), jnp.bfloat16),
        in_specs=[VMEM] * len(flat),
        out_specs=VMEM,
        compiler_params=params(),
        name="finish_rows",
    )(*flat)


def reorder_kernel(tiles_held, owner, received, out):
    for t in range(owner.shape[0]):
        at = owner[t]
        start = pl.multiple_of((at % tiles_held) * TILE, TILE)
        out[:, t * TILE:(t + 1) * TILE] = received[at // tiles_held, :, pl.ds(start, TILE)]


def reorder(owner, received):
    columns, rows, width = received.shape
    return pl.pallas_call(
        functools.partial(reorder_kernel, width // TILE),
        out_shape=jax.ShapeDtypeStruct((rows, columns * width), received.dtype),
        in_specs=[SMEM, VMEM],
        out_specs=VMEM,
        compiler_params=params(),
        name="reorder_tiles",
    )(owner, received)


def swap(x, axis, flip):
    return lax.ppermute(x, axis, [(i, i ^ flip) for i in range(lax.axis_size(axis))])


def body(amplitudes, integrals, wanted, owner):
    columns = lax.axis_size("col")
    parts = lax.axis_size("row")
    ys = parts // CORES
    pairs = amplitudes.shape[0]
    per_source = amplitudes.shape[1] // TILE
    per_device = pairs // (columns * parts)
    top = columns // 2
    low = list(range(1, top))
    b = max(per_device, 16)
    units = pairs // (parts * b)
    if b != per_device:
        amplitudes = amplitudes.reshape(units, columns // units, parts, per_device, -1).transpose(0, 2, 1, 3, 4)
    order = halving_order(ys)
    slots = [order[:ys // 2], order[ys // 2:]]
    first = units * FIRST // 4
    bounds = [(0, first), (first, units)] if first < units else [(0, units)]

    def whole(x):
        return x.reshape(units, ys, b, -1)

    def flat(x):
        return x.reshape(units * ys * b, -1)

    def spread(picked):
        return [swap(x, "col", f).reshape(CORES, CAP, -1, ys, b, TILE) for x, f in zip(picked, low)]

    mine, theirs = split(amplitudes.reshape(units, ys, CORES, b, -1))
    own = [mine, swap(theirs, "row", 1)]
    early = swap(mine, "col", top)
    picked = select(wanted, [flat(x) for x in own], per_source, 0, low)
    nearby = spread(picked)
    mirrors = [early, swap(own[1], "col", top)]
    blocks = arrange(wanted, [integrals, swap(integrals, "row", 1)], per_source, top)
    late_wanted, *blocks = lax.optimization_barrier((wanted, *blocks))
    choices = choice(late_wanted, per_source, top, low, amplitudes.dtype)
    *mirrors, early_block, far_block, choices = lax.optimization_barrier((*mirrors, *blocks, choices))
    mirrors = [whole(x) for x in mirrors]
    height = ys * b
    passed = pass_on([flat(x) for x in mirrors], choices, [(lo * height, hi * height) for lo, hi in bounds])
    groups = [passed[n:n + len(low)] for n in range(0, len(passed), len(low))]
    far = [spread(groups[0])]
    sums = contract(own + nearby + mirrors, early_block, [(at, flips) for at in bounds for flips in slots])
    for group in groups[1:]:
        far.append(spread(group))
    pieces = []
    for n, (lo, hi) in enumerate(bounds):
        span = (0, hi - lo)
        send, = contract(far[n], far_block, [(span, slots[0])], sums[2 * n:2 * n + 1], coded=True)
        keep, = contract(far[n], far_block, [(span, slots[1])], sums[2 * n + 1:2 * n + 2])
        bit = CORES
        while True:
            arrived = swap(send, "row", bit)
            bit *= 2
            if bit == parts:
                break
            send, keep = fold(keep, arrived)
        pieces.append((keep, arrived))
    held = finish(pieces).reshape(columns, per_device, -1)
    exchanged = lax.all_to_all(held, "col", split_axis=0, concat_axis=0, tiled=True)
    return reorder(owner, exchanged)


def solution(mesh):
    in_specs = (P(None, ("col", "row")), P("row", "col"), P(), P())
    out_specs = P(("col", "row"), None)
    return jax.shard_map(body, mesh=mesh, in_specs=in_specs, out_specs=out_specs, check_vma=False)
```

```python
import functools

import jax
import jax.numpy as jnp
from jax import lax
from jax.experimental import pallas as pl
from jax.experimental.pallas import tpu as pltpu
from jax.sharding import PartitionSpec as P

TILE = 128
CAP = 2
CORES = 2
FIRST = 2
SMALL = 8 * 1024 * 1024
LEAST = 2.0 ** -125
STEPS = 32766.0
ANY = pl.BlockSpec(memory_space=pl.ANY)
SMEM = pl.BlockSpec(memory_space=pltpu.SMEM)
VMEM = pl.BlockSpec(memory_space=pltpu.VMEM)


def params(size=0):
    return pltpu.CompilerParams(vmem_limit_bytes=size + SMALL)


def halving_order(count):
    bits = count.bit_length() - 1
    return [int(format(count - 1 - j, "b").zfill(bits)[::-1], 2) for j in range(count)] if bits else [0]


def split_kernel(amps, mine, theirs, sem):
    core = lax.axis_index("row") % CORES
    copies = [
        pltpu.make_async_copy(amps.at[:, :, core], mine, sem.at[0]),
        pltpu.make_async_copy(amps.at[:, :, 1 - core], theirs, sem.at[1]),
    ]
    for copy in copies:
        copy.start()
    for copy in copies:
        copy.wait()


def split(amps):
    shape = jax.ShapeDtypeStruct(amps.shape[:2] + amps.shape[3:], amps.dtype)
    return pl.pallas_call(
        split_kernel,
        out_shape=[shape, shape],
        in_specs=[ANY],
        out_specs=[ANY, ANY],
        scratch_shapes=[pltpu.SemaphoreType.DMA((2,))],
        compiler_params=params(),
        name="split_rows",
    )(amps)


def select_kernel(per_source, away, flips, wanted, *rest):
    groups, outs, sem = rest[:CORES], rest[CORES:-1], rest[-1]
    me, row = lax.axis_index("col"), lax.axis_index("row")
    length = wanted.shape[2]
    source = me ^ away
    copies = []
    for n, flip in enumerate(flips):
        other = me ^ flip
        for g in range(CORES):

            def step(k, found):
                first, second, count = found
                w = wanted[other, row ^ g, k]
                mine = w // per_source == source
                tile = w % per_source
                first = jnp.where(mine & (count == 0), tile, first)
                second = jnp.where(mine & (count == 1), tile, second)
                return first, second, count + mine.astype(jnp.int32)

            zero = jnp.int32(0)
            found = lax.fori_loop(0, length, step, (zero, zero, zero), unroll=length <= 8)
            for slot in range(CAP):
                start = pl.multiple_of(found[slot] * TILE, TILE)
                copy = pltpu.make_async_copy(groups[g].at[:, pl.ds(start, TILE)], outs[n].at[g, slot], sem.at[n, g, slot])
                copy.start()
                copies.append(copy)
    for copy in copies:
        copy.wait()


def select(wanted, groups, per_source, away, flips):
    rows = groups[0].shape[0]
    shape = jax.ShapeDtypeStruct((CORES, CAP, rows, TILE), groups[0].dtype)
    return pl.pallas_call(
        functools.partial(select_kernel, per_source, away, flips),
        out_shape=[shape] * len(flips),
        in_specs=[SMEM] + [ANY] * CORES,
        out_specs=[ANY] * len(flips),
        scratch_shapes=[pltpu.SemaphoreType.DMA((len(flips), CORES, CAP))],
        compiler_params=params(),
        name="select_tiles",
    )(wanted, *groups)


def choice_kernel(per_source, away, flips, wanted, *outs):
    me, row = lax.axis_index("col"), lax.axis_index("row")
    length = wanted.shape[2]
    source = me ^ away
    one = (lax.broadcasted_iota(jnp.int32, (TILE, TILE), 0) == lax.broadcasted_iota(jnp.int32, (TILE, TILE), 1)).astype(outs[0].dtype)
    for g, out in enumerate(outs):
        out[...] = jnp.zeros_like(out)
        for n, flip in enumerate(flips):
            other = me ^ flip

            def step(k, count):
                w = wanted[other, row ^ g, k]
                mine = w // per_source == source
                at = pl.ds(pl.multiple_of((w % per_source) * TILE, TILE), TILE)
                for slot in range(CAP):

                    @pl.when(mine & (count == slot))
                    def _():
                        low = (n * CAP + slot) * TILE
                        out[at, low:low + TILE] = one

                return count + mine.astype(jnp.int32)

            lax.fori_loop(0, length, step, jnp.int32(0))


def choice(wanted, per_source, away, flips, dtype):
    shape = jax.ShapeDtypeStruct((per_source * TILE, len(flips) * CAP * TILE), dtype)
    return pl.pallas_call(
        functools.partial(choice_kernel, per_source, away, flips),
        out_shape=[shape] * CORES,
        in_specs=[SMEM],
        out_specs=[VMEM] * CORES,
        compiler_params=params(4 * shape.size * CORES),
        name="choice_matrices",
    )(wanted)


def pass_on_kernel(ranges, *refs):
    groups, choices, outs = refs[:CORES], refs[CORES:2 * CORES], refs[2 * CORES:]
    count = len(outs) // len(ranges)
    for g in range(CORES):
        x = jnp.dot(groups[g][...], choices[g][...], preferred_element_type=jnp.float32).astype(outs[0].dtype)
        for m, (start, stop) in enumerate(ranges):
            for n in range(count):
                for slot in range(CAP):
                    low = (n * CAP + slot) * TILE
                    outs[m * count + n][g, slot] = x[start:stop, low:low + TILE]


def pass_on(groups, choices, ranges):
    rows, chosen = groups[0].shape[0], choices[0].shape[1]
    shapes = [jax.ShapeDtypeStruct((CORES, CAP, stop - start, TILE), groups[0].dtype) for start, stop in ranges for _ in range(chosen // (CAP * TILE))]
    size = sum(2 * x.size for x in (*groups, *choices)) + 4 * CORES * rows * chosen * 2
    return pl.pallas_call(
        functools.partial(pass_on_kernel, ranges),
        out_shape=shapes,
        in_specs=[VMEM] * (2 * CORES),
        out_specs=[VMEM] * len(shapes),
        compiler_params=params(size),
        name="pass_on_tiles",
    )(*groups, *choices)


def arrange_kernel(per_source, top, wanted, *refs):
    blocks, (early, far) = refs[:CORES], refs[CORES:]
    me, row = lax.axis_index("col"), lax.axis_index("row")
    length = wanted.shape[2]
    for part in (early, far):
        part[...] = jnp.zeros_like(part)
    near_base = CORES * per_source
    whole_base = near_base + CORES * CAP * (top - 1)
    for g in range(CORES):

        def place(k, carry):
            w = wanted[me, row ^ g, k]
            source = w // per_source
            slot = lax.fori_loop(0, k, lambda i, n: n + (wanted[me, row ^ g, i] // per_source == source).astype(jnp.int32), jnp.int32(0))
            away, tile = source ^ me, w % per_source
            passed = CAP * (CORES * (lax.rem(away, top) - 1) + g) + slot
            rows = blocks[g][pl.ds(pl.multiple_of(k * TILE, TILE), TILE)]

            def put(part, condition, at):
                @pl.when(condition)
                def _():
                    part[pl.ds(pl.multiple_of(at * TILE, TILE), TILE)] = rows

            put(early, away == 0, g * per_source + tile)
            put(early, (away > 0) & (away < top), near_base + passed)
            put(early, away == top, whole_base + g * per_source + tile)
            put(far, away > top, passed)
            return carry

        lax.fori_loop(0, length, place, 0)


def arrange(wanted, blocks, per_source, top):
    depth, width = blocks[0].shape
    passed = CORES * CAP * (top - 1)
    depths = [TILE * n for n in (2 * CORES * per_source + passed, passed)]
    part = width if depth <= 1024 else width // 4
    size = 4 * part * (CORES * depth + sum(depths))
    return pl.pallas_call(
        functools.partial(arrange_kernel, per_source, top),
        grid=(width // part,),
        out_shape=[jax.ShapeDtypeStruct((n, width), blocks[0].dtype) for n in depths],
        in_specs=[SMEM] + [pl.BlockSpec((depth, part), lambda n: (0, n))] * CORES,
        out_specs=[pl.BlockSpec((n, part), lambda n: (0, n)) for n in depths],
        compiler_params=params(size),
        name="arrange_block",
    )(wanted, *blocks)


def code(x):
    most = jnp.max(jnp.abs(x), axis=1, keepdims=True)
    power = jnp.clip(jnp.ceil(jnp.log2(jnp.maximum(most, LEAST))), -125.0, 120.0)
    scaled = jnp.floor(x * jnp.exp2(-power) * STEPS + 0.5)
    scaled = jnp.clip(scaled, -32767.0, 32767.0).astype(jnp.int32).astype(jnp.int16)
    powers = jnp.broadcast_to(power, (x.shape[0], TILE)).astype(jnp.int32).astype(jnp.int16)
    return scaled, powers


def decode(coded):
    width = coded.shape[1] - TILE
    power = coded[:, width:].astype(jnp.int32).astype(jnp.float32)[:, :1]
    return coded[:, :width].astype(jnp.int32).astype(jnp.float32) * (1 / STEPS) * jnp.exp2(power)


def steps(rows):
    size = 64 if rows % 64 == 0 else 32 if rows % 32 == 0 else 16
    return [slice(start, start + size) for start in range(0, rows, size)]


def put_coded(out, at, x):
    width = x.shape[1]
    out[at, :width], out[at, width:] = code(x)


def fill(left, source, units, flip, depth, at):
    y = (lax.axis_index("row") // CORES) ^ flip
    span = units[1] - units[0]
    low = units[0] if source.shape[-4] > span else 0
    rows = pl.ds(at, span * source.shape[-2])
    if len(source.shape) == 4:
        tiles = [source[low:low + span, y]]
    else:
        tiles = [source[g, slot, low:low + span, y] for g in range(source.shape[0]) for slot in range(CAP)]
    for tile in tiles:
        width = tile.shape[-1]
        left[rows, depth:depth + width] = tile.reshape(-1, width)
        depth += width
    return depth


def contract_kernel(count, pieces, coded, *refs):
    sources, block = refs[:count], refs[count]
    before, outs, left = refs[count + 1:-1 - len(pieces)], refs[-1 - len(pieces):-1], refs[-1]
    base = 0
    for n, (units, flips) in enumerate(pieces):
        rows = outs[n].shape[0] // len(flips)
        for j, flip in enumerate(flips):
            depth = 0
            for source in sources:
                depth = fill(left, source, units, flip, depth, base + j * rows)
        base += outs[n].shape[0]
    product = jnp.dot(left[...], block[...], preferred_element_type=jnp.float32)
    base = 0
    for n in range(len(pieces)):
        rows = outs[n].shape[0]
        x = product[base:base + rows]
        base += rows
        if before:
            x = before[n][...] + x
        if coded:
            put_coded(outs[n], slice(None), x)
        else:
            outs[n][...] = x


def contract(sources, block, pieces, before=(), coded=False):
    depth, width = block.shape
    rows = [(units[1] - units[0]) * sources[0].shape[-2] * len(flips) for units, flips in pieces]
    if coded:
        shapes = [jax.ShapeDtypeStruct((n, width + TILE), jnp.int16) for n in rows]
    else:
        shapes = [jax.ShapeDtypeStruct((n, width), jnp.float32) for n in rows]
    size = 2 * depth * (width + sum(rows)) + 16 * width * sum(rows) + sum(2 * x.size for x in sources)
    return pl.pallas_call(
        functools.partial(contract_kernel, len(sources), pieces, coded),
        out_shape=shapes,
        in_specs=[VMEM] * (len(sources) + 1 + len(before)),
        out_specs=[VMEM] * len(shapes),
        scratch_shapes=[pltpu.VMEM((sum(rows), depth), block.dtype)],
        compiler_params=params(size),
        name="contract_tiles",
    )(*sources, block, *before)


def fold_kernel(keep, arrived, send, kept):
    half = kept.shape[0]
    for at in steps(half):
        put_coded(send, at, keep[at] + decode(arrived[at]))
    for at in steps(half):
        low = slice(at.start + half, at.stop + half)
        kept[at] = keep[low] + decode(arrived[low])


def fold(keep, arrived):
    half, width = keep.shape[0] // 2, keep.shape[1]
    return pl.pallas_call(
        fold_kernel,
        out_shape=[jax.ShapeDtypeStruct((half, width + TILE), jnp.int16), jax.ShapeDtypeStruct((half, width), jnp.float32)],
        in_specs=[VMEM, VMEM],
        out_specs=[VMEM, VMEM],
        compiler_params=params(),
        name="fold_rows",
    )(keep, arrived)


def finish_kernel(*refs):
    out, base = refs[-1], 0
    for keep, arrived in zip(refs[:-1:2], refs[1:-1:2]):
        for at in steps(keep.shape[0]):
            out[base + at.start:base + at.stop] = (keep[at] + decode(arrived[at])).astype(out.dtype)
        base += keep.shape[0]


def finish(pieces):
    flat = [x for piece in pieces for x in piece]
    rows = sum(keep.shape[0] for keep, _ in pieces)
    return pl.pallas_call(
        finish_kernel,
        out_shape=jax.ShapeDtypeStruct((rows, flat[0].shape[1]), jnp.bfloat16),
        in_specs=[VMEM] * len(flat),
        out_specs=VMEM,
        compiler_params=params(),
        name="finish_rows",
    )(*flat)


def reorder_kernel(tiles_held, owner, received, out):
    for t in range(owner.shape[0]):
        at = owner[t]
        start = pl.multiple_of((at % tiles_held) * TILE, TILE)
        out[:, t * TILE:(t + 1) * TILE] = received[at // tiles_held, :, pl.ds(start, TILE)]


def reorder(owner, received):
    columns, rows, width = received.shape
    return pl.pallas_call(
        functools.partial(reorder_kernel, width // TILE),
        out_shape=jax.ShapeDtypeStruct((rows, columns * width), received.dtype),
        in_specs=[SMEM, VMEM],
        out_specs=VMEM,
        compiler_params=params(),
        name="reorder_tiles",
    )(owner, received)


def swap(x, axis, flip):
    return lax.ppermute(x, axis, [(i, i ^ flip) for i in range(lax.axis_size(axis))])


def body(amplitudes, integrals, wanted, owner):
    columns = lax.axis_size("col")
    parts = lax.axis_size("row")
    ys = parts // CORES
    pairs = amplitudes.shape[0]
    per_source = amplitudes.shape[1] // TILE
    per_device = pairs // (columns * parts)
    top = columns // 2
    low = list(range(1, top))
    b = max(per_device, 16)
    units = pairs // (parts * b)
    if b != per_device:
        amplitudes = amplitudes.reshape(units, columns // units, parts, per_device, -1).transpose(0, 2, 1, 3, 4)
    order = halving_order(ys)
    slots = [order[:ys // 2], order[ys // 2:]]
    first = units * FIRST // 4
    bounds = [(0, first), (first, units)] if first < units else [(0, units)]

    def whole(x):
        return x.reshape(units, ys, b, -1)

    def flat(x):
        return x.reshape(units * ys * b, -1)

    def spread(picked):
        return [swap(x, "col", f).reshape(CORES, CAP, -1, ys, b, TILE) for x, f in zip(picked, low)]

    mine, theirs = split(amplitudes.reshape(units, ys, CORES, b, -1))
    own = [mine, swap(theirs, "row", 1)]
    early = swap(mine, "col", top)
    picked = select(wanted, [flat(x) for x in own], per_source, 0, low)
    nearby = spread(picked)
    mirrors = [early, swap(own[1], "col", top)]
    blocks = arrange(wanted, [integrals, swap(integrals, "row", 1)], per_source, top)
    late_wanted, *blocks = lax.optimization_barrier((wanted, *blocks))
    choices = choice(late_wanted, per_source, top, low, amplitudes.dtype)
    *mirrors, early_block, far_block, choices, nearby[1] = lax.optimization_barrier((*mirrors, *blocks, choices, nearby[1]))
    mirrors = [whole(x) for x in mirrors]
    height = ys * b
    passed = pass_on([flat(x) for x in mirrors], choices, [(lo * height, hi * height) for lo, hi in bounds])
    groups = [passed[n:n + len(low)] for n in range(0, len(passed), len(low))]
    far = [spread(groups[0])]
    sums = contract(own + nearby + mirrors, early_block, [(at, flips) for at in bounds for flips in slots])
    for group in groups[1:]:
        far.append(spread(group))
    pieces = []
    for n, (lo, hi) in enumerate(bounds):
        span = (0, hi - lo)
        send, = contract(far[n], far_block, [(span, slots[0])], sums[2 * n:2 * n + 1], coded=True)
        keep, = contract(far[n], far_block, [(span, slots[1])], sums[2 * n + 1:2 * n + 2])
        bit = CORES
        while True:
            arrived = swap(send, "row", bit)
            bit *= 2
            if bit == parts:
                break
            send, keep = fold(keep, arrived)
        pieces.append((keep, arrived))
    held = finish(pieces).reshape(columns, per_device, -1)
    exchanged = lax.all_to_all(held, "col", split_axis=0, concat_axis=0, tiled=True)
    return reorder(owner, exchanged)


def solution(mesh):
    in_specs = (P(None, ("col", "row")), P("row", "col"), P(), P())
    out_specs = P(("col", "row"), None)
    return jax.shard_map(body, mesh=mesh, in_specs=in_specs, out_specs=out_specs, check_vma=False)
```

```python
import functools

import jax
import jax.numpy as jnp
from jax import lax
from jax.experimental import pallas as pl
from jax.experimental.pallas import tpu as pltpu
from jax.sharding import PartitionSpec as P

TILE = 128
CAP = 2
CORES = 2
FIRST = 2
SMALL = 8 * 1024 * 1024
LEAST = 2.0 ** -125
STEPS = 32766.0
ANY = pl.BlockSpec(memory_space=pl.ANY)
SMEM = pl.BlockSpec(memory_space=pltpu.SMEM)
VMEM = pl.BlockSpec(memory_space=pltpu.VMEM)


def params(size=0):
    return pltpu.CompilerParams(vmem_limit_bytes=size + SMALL)


def halving_order(count):
    bits = count.bit_length() - 1
    return [int(format(count - 1 - j, "b").zfill(bits)[::-1], 2) for j in range(count)] if bits else [0]


def split_kernel(amps, mine, theirs, sem):
    core = lax.axis_index("row") % CORES
    copies = [
        pltpu.make_async_copy(amps.at[:, :, core], mine, sem.at[0]),
        pltpu.make_async_copy(amps.at[:, :, 1 - core], theirs, sem.at[1]),
    ]
    for copy in copies:
        copy.start()
    for copy in copies:
        copy.wait()


def split(amps):
    shape = jax.ShapeDtypeStruct(amps.shape[:2] + amps.shape[3:], amps.dtype)
    return pl.pallas_call(
        split_kernel,
        out_shape=[shape, shape],
        in_specs=[ANY],
        out_specs=[ANY, ANY],
        scratch_shapes=[pltpu.SemaphoreType.DMA((2,))],
        compiler_params=params(),
        name="split_rows",
    )(amps)


def select_kernel(per_source, away, flips, wanted, *rest):
    groups, outs, sem = rest[:CORES], rest[CORES:-1], rest[-1]
    me, row = lax.axis_index("col"), lax.axis_index("row")
    length = wanted.shape[2]
    source = me ^ away
    copies = []
    for n, flip in enumerate(flips):
        other = me ^ flip
        for g in range(CORES):
            first = second = count = jnp.int32(0)
            for k in range(length):
                w = wanted[other, row ^ g, k]
                mine = w // per_source == source
                tile = w % per_source
                first = jnp.where(mine & (count == 0), tile, first)
                second = jnp.where(mine & (count == 1), tile, second)
                count = count + mine.astype(jnp.int32)
            found = (first, second)
            for slot in range(CAP):
                start = pl.multiple_of(found[slot] * TILE, TILE)
                copy = pltpu.make_async_copy(groups[g].at[:, pl.ds(start, TILE)], outs[n].at[g, slot], sem.at[n, g, slot])
                copy.start()
                copies.append(copy)
    for copy in copies:
        copy.wait()


def select(wanted, groups, per_source, away, flips):
    rows = groups[0].shape[0]
    shape = jax.ShapeDtypeStruct((CORES, CAP, rows, TILE), groups[0].dtype)
    return pl.pallas_call(
        functools.partial(select_kernel, per_source, away, flips),
        out_shape=[shape] * len(flips),
        in_specs=[VMEM] + [ANY] * CORES,
        out_specs=[ANY] * len(flips),
        scratch_shapes=[pltpu.SemaphoreType.DMA((len(flips), CORES, CAP))],
        compiler_params=params(),
        name="select_tiles",
    )(wanted, *groups)


def choice_kernel(per_source, away, flips, wanted, *outs):
    me, row = lax.axis_index("col"), lax.axis_index("row")
    length = wanted.shape[2]
    source = me ^ away
    one = (lax.broadcasted_iota(jnp.int32, (TILE, TILE), 0) == lax.broadcasted_iota(jnp.int32, (TILE, TILE), 1)).astype(outs[0].dtype)
    for g, out in enumerate(outs):
        out[...] = jnp.zeros_like(out)
        for n, flip in enumerate(flips):
            other = me ^ flip

            def step(k, count):
                w = wanted[other, row ^ g, k]
                mine = w // per_source == source
                at = pl.ds(pl.multiple_of((w % per_source) * TILE, TILE), TILE)
                for slot in range(CAP):

                    @pl.when(mine & (count == slot))
                    def _():
                        low = (n * CAP + slot) * TILE
                        out[at, low:low + TILE] = one

                return count + mine.astype(jnp.int32)

            lax.fori_loop(0, length, step, jnp.int32(0))


def choice(wanted, per_source, away, flips, dtype):
    shape = jax.ShapeDtypeStruct((per_source * TILE, len(flips) * CAP * TILE), dtype)
    return pl.pallas_call(
        functools.partial(choice_kernel, per_source, away, flips),
        out_shape=[shape] * CORES,
        in_specs=[SMEM],
        out_specs=[VMEM] * CORES,
        compiler_params=params(4 * shape.size * CORES),
        name="choice_matrices",
    )(wanted)


def pass_on_kernel(ranges, *refs):
    groups, choices, outs = refs[:CORES], refs[CORES:2 * CORES], refs[2 * CORES:]
    count = len(outs) // len(ranges)
    for g in range(CORES):
        x = jnp.dot(groups[g][...], choices[g][...], preferred_element_type=jnp.float32).astype(outs[0].dtype)
        for m, (start, stop) in enumerate(ranges):
            for n in range(count):
                for slot in range(CAP):
                    low = (n * CAP + slot) * TILE
                    outs[m * count + n][g, slot] = x[start:stop, low:low + TILE]


def pass_on(groups, choices, ranges):
    rows, chosen = groups[0].shape[0], choices[0].shape[1]
    shapes = [jax.ShapeDtypeStruct((CORES, CAP, stop - start, TILE), groups[0].dtype) for start, stop in ranges for _ in range(chosen // (CAP * TILE))]
    size = sum(2 * x.size for x in (*groups, *choices)) + 4 * CORES * rows * chosen * 2
    return pl.pallas_call(
        functools.partial(pass_on_kernel, ranges),
        out_shape=shapes,
        in_specs=[VMEM] * (2 * CORES),
        out_specs=[VMEM] * len(shapes),
        compiler_params=params(size),
        name="pass_on_tiles",
    )(*groups, *choices)


def arrange_kernel(per_source, top, wanted, *refs):
    blocks, (early, far) = refs[:CORES], refs[CORES:]
    me, row = lax.axis_index("col"), lax.axis_index("row")
    length = wanted.shape[2]
    for part in (early, far):
        part[...] = jnp.zeros_like(part)
    near_base = CORES * per_source
    whole_base = near_base + CORES * CAP * (top - 1)
    for g in range(CORES):

        def place(k, carry):
            w = wanted[me, row ^ g, k]
            source = w // per_source
            slot = lax.fori_loop(0, k, lambda i, n: n + (wanted[me, row ^ g, i] // per_source == source).astype(jnp.int32), jnp.int32(0))
            away, tile = source ^ me, w % per_source
            passed = CAP * (CORES * (lax.rem(away, top) - 1) + g) + slot
            rows = blocks[g][pl.ds(pl.multiple_of(k * TILE, TILE), TILE)]

            def put(part, condition, at):
                @pl.when(condition)
                def _():
                    part[pl.ds(pl.multiple_of(at * TILE, TILE), TILE)] = rows

            put(early, away == 0, g * per_source + tile)
            put(early, (away > 0) & (away < top), near_base + passed)
            put(early, away == top, whole_base + g * per_source + tile)
            put(far, away > top, passed)
            return carry

        lax.fori_loop(0, length, place, 0)


def arrange(wanted, blocks, per_source, top):
    depth, width = blocks[0].shape
    passed = CORES * CAP * (top - 1)
    depths = [TILE * n for n in (2 * CORES * per_source + passed, passed)]
    part = width if depth <= 1024 else width // 4
    size = 4 * part * (CORES * depth + sum(depths))
    return pl.pallas_call(
        functools.partial(arrange_kernel, per_source, top),
        grid=(width // part,),
        out_shape=[jax.ShapeDtypeStruct((n, width), blocks[0].dtype) for n in depths],
        in_specs=[SMEM] + [pl.BlockSpec((depth, part), lambda n: (0, n))] * CORES,
        out_specs=[pl.BlockSpec((n, part), lambda n: (0, n)) for n in depths],
        compiler_params=params(size),
        name="arrange_block",
    )(wanted, *blocks)


def code(x):
    most = jnp.max(jnp.abs(x), axis=1, keepdims=True)
    power = jnp.clip(jnp.ceil(jnp.log2(jnp.maximum(most, LEAST))), -125.0, 120.0)
    scaled = jnp.floor(x * jnp.exp2(-power) * STEPS + 0.5)
    scaled = jnp.clip(scaled, -32767.0, 32767.0).astype(jnp.int32).astype(jnp.int16)
    powers = jnp.broadcast_to(power, (x.shape[0], TILE)).astype(jnp.int32).astype(jnp.int16)
    return scaled, powers


def decode(coded):
    width = coded.shape[1] - TILE
    power = coded[:, width:].astype(jnp.int32).astype(jnp.float32)[:, :1]
    return coded[:, :width].astype(jnp.int32).astype(jnp.float32) * (1 / STEPS) * jnp.exp2(power)


def steps(rows):
    size = 64 if rows % 64 == 0 else 32 if rows % 32 == 0 else 16
    return [slice(start, start + size) for start in range(0, rows, size)]


def put_coded(out, at, x):
    width = x.shape[1]
    out[at, :width], out[at, width:] = code(x)


def fill(left, source, units, flip, depth, at):
    y = (lax.axis_index("row") // CORES) ^ flip
    span = units[1] - units[0]
    low = units[0] if source.shape[-4] > span else 0
    rows = pl.ds(at, span * source.shape[-2])
    if len(source.shape) == 4:
        tiles = [source[low:low + span, y]]
    else:
        tiles = [source[g, slot, low:low + span, y] for g in range(source.shape[0]) for slot in range(CAP)]
    for tile in tiles:
        width = tile.shape[-1]
        left[rows, depth:depth + width] = tile.reshape(-1, width)
        depth += width
    return depth


def contract_kernel(count, pieces, coded, *refs):
    sources, block = refs[:count], refs[count]
    before, outs, left = refs[count + 1:-1 - len(pieces)], refs[-1 - len(pieces):-1], refs[-1]
    base = 0
    for n, (units, flips) in enumerate(pieces):
        rows = outs[n].shape[0] // len(flips)
        for j, flip in enumerate(flips):
            depth = 0
            for source in sources:
                depth = fill(left, source, units, flip, depth, base + j * rows)
        base += outs[n].shape[0]
    product = jnp.dot(left[...], block[...], preferred_element_type=jnp.float32)
    base = 0
    for n in range(len(pieces)):
        rows = outs[n].shape[0]
        x = product[base:base + rows]
        base += rows
        if before:
            x = before[n][...] + x
        if coded:
            put_coded(outs[n], slice(None), x)
        else:
            outs[n][...] = x


def contract(sources, block, pieces, before=(), coded=False):
    depth, width = block.shape
    rows = [(units[1] - units[0]) * sources[0].shape[-2] * len(flips) for units, flips in pieces]
    if coded:
        shapes = [jax.ShapeDtypeStruct((n, width + TILE), jnp.int16) for n in rows]
    else:
        shapes = [jax.ShapeDtypeStruct((n, width), jnp.float32) for n in rows]
    size = 2 * depth * (width + sum(rows)) + 16 * width * sum(rows) + sum(2 * x.size for x in sources)
    return pl.pallas_call(
        functools.partial(contract_kernel, len(sources), pieces, coded),
        out_shape=shapes,
        in_specs=[VMEM] * (len(sources) + 1 + len(before)),
        out_specs=[VMEM] * len(shapes),
        scratch_shapes=[pltpu.VMEM((sum(rows), depth), block.dtype)],
        compiler_params=params(size),
        name="contract_tiles",
    )(*sources, block, *before)


def fold_kernel(keep, arrived, send, kept):
    half = kept.shape[0]
    for at in steps(half):
        put_coded(send, at, keep[at] + decode(arrived[at]))
    for at in steps(half):
        low = slice(at.start + half, at.stop + half)
        kept[at] = keep[low] + decode(arrived[low])


def fold(keep, arrived):
    half, width = keep.shape[0] // 2, keep.shape[1]
    return pl.pallas_call(
        fold_kernel,
        out_shape=[jax.ShapeDtypeStruct((half, width + TILE), jnp.int16), jax.ShapeDtypeStruct((half, width), jnp.float32)],
        in_specs=[VMEM, VMEM],
        out_specs=[VMEM, VMEM],
        compiler_params=params(),
        name="fold_rows",
    )(keep, arrived)


def finish_kernel(*refs):
    out, base = refs[-1], 0
    for keep, arrived in zip(refs[:-1:2], refs[1:-1:2]):
        for at in steps(keep.shape[0]):
            out[base + at.start:base + at.stop] = (keep[at] + decode(arrived[at])).astype(out.dtype)
        base += keep.shape[0]


def finish(pieces):
    flat = [x for piece in pieces for x in piece]
    rows = sum(keep.shape[0] for keep, _ in pieces)
    return pl.pallas_call(
        finish_kernel,
        out_shape=jax.ShapeDtypeStruct((rows, flat[0].shape[1]), jnp.bfloat16),
        in_specs=[VMEM] * len(flat),
        out_specs=VMEM,
        compiler_params=params(),
        name="finish_rows",
    )(*flat)


def reorder_kernel(tiles_held, owner, received, out):
    for t in range(owner.shape[1]):
        at = owner[0, t]
        start = pl.multiple_of((at % tiles_held) * TILE, TILE)
        out[:, t * TILE:(t + 1) * TILE] = received[at // tiles_held, :, pl.ds(start, TILE)]


def reorder(owner, received):
    columns, rows, width = received.shape
    return pl.pallas_call(
        functools.partial(reorder_kernel, width // TILE),
        out_shape=jax.ShapeDtypeStruct((rows, columns * width), received.dtype),
        in_specs=[VMEM, VMEM],
        out_specs=VMEM,
        compiler_params=params(),
        name="reorder_tiles",
    )(owner.reshape(1, -1), received)


def swap(x, axis, flip):
    return lax.ppermute(x, axis, [(i, i ^ flip) for i in range(lax.axis_size(axis))])


def body(amplitudes, integrals, wanted, owner):
    columns = lax.axis_size("col")
    parts = lax.axis_size("row")
    ys = parts // CORES
    pairs = amplitudes.shape[0]
    per_source = amplitudes.shape[1] // TILE
    per_device = pairs // (columns * parts)
    top = columns // 2
    low = list(range(1, top))
    b = max(per_device, 16)
    units = pairs // (parts * b)
    if b != per_device:
        amplitudes = amplitudes.reshape(units, columns // units, parts, per_device, -1).transpose(0, 2, 1, 3, 4)
    order = halving_order(ys)
    slots = [order[:ys // 2], order[ys // 2:]]
    first = units * FIRST // 4
    bounds = [(0, first), (first, units)] if first < units else [(0, units)]

    def whole(x):
        return x.reshape(units, ys, b, -1)

    def flat(x):
        return x.reshape(units * ys * b, -1)

    def spread(picked):
        return [swap(x, "col", f).reshape(CORES, CAP, -1, ys, b, TILE) for x, f in zip(picked, low)]

    mine, theirs = split(amplitudes.reshape(units, ys, CORES, b, -1))
    own = [mine, swap(theirs, "row", 1)]
    early = swap(mine, "col", top)
    picked = select(wanted, [flat(x) for x in own], per_source, 0, low)
    nearby = spread(picked)
    mirrors = [early, swap(own[1], "col", top)]
    blocks = arrange(wanted, [integrals, swap(integrals, "row", 1)], per_source, top)
    late_wanted, *blocks = lax.optimization_barrier((wanted, *blocks))
    choices = choice(late_wanted, per_source, top, low, amplitudes.dtype)
    *mirrors, early_block, far_block, choices, nearby[top // 2 - 1] = lax.optimization_barrier((*mirrors, *blocks, choices, nearby[top // 2 - 1]))
    mirrors = [whole(x) for x in mirrors]
    height = ys * b
    passed = pass_on([flat(x) for x in mirrors], choices, [(lo * height, hi * height) for lo, hi in bounds])
    groups = [passed[n:n + len(low)] for n in range(0, len(passed), len(low))]
    far = [spread(groups[0])]
    sums = contract(own + nearby + mirrors, early_block, [(at, flips) for at in bounds for flips in slots])
    for group in groups[1:]:
        far.append(spread(group))
    pieces = []
    for n, (lo, hi) in enumerate(bounds):
        span = (0, hi - lo)
        send, = contract(far[n], far_block, [(span, slots[0])], sums[2 * n:2 * n + 1], coded=True)
        keep, = contract(far[n], far_block, [(span, slots[1])], sums[2 * n + 1:2 * n + 2])
        bit = CORES
        while True:
            arrived = swap(send, "row", bit)
            bit *= 2
            if bit == parts:
                break
            send, keep = fold(keep, arrived)
        pieces.append((keep, arrived))
    held = finish(pieces).reshape(columns, per_device, -1)
    exchanged = lax.all_to_all(held, "col", split_axis=0, concat_axis=0, tiled=True)
    return reorder(owner, exchanged)


def solution(mesh):
    in_specs = (P(None, ("col", "row")), P("row", "col"), P(), P())
    out_specs = P(("col", "row"), None)
    return jax.shard_map(body, mesh=mesh, in_specs=in_specs, out_specs=out_specs, check_vma=False)
```

```python
import functools

import jax
import jax.numpy as jnp
from jax import lax
from jax.experimental import pallas as pl
from jax.experimental.pallas import tpu as pltpu
from jax.sharding import PartitionSpec as P

TILE = 128
CAP = 2
CORES = 2
FIRST = 2
SMALL = 8 * 1024 * 1024
LEAST = 2.0 ** -125
STEPS = 32766.0
ANY = pl.BlockSpec(memory_space=pl.ANY)
SMEM = pl.BlockSpec(memory_space=pltpu.SMEM)
VMEM = pl.BlockSpec(memory_space=pltpu.VMEM)


def params(size=0):
    return pltpu.CompilerParams(vmem_limit_bytes=size + SMALL)


def halving_order(count):
    bits = count.bit_length() - 1
    return [int(format(count - 1 - j, "b").zfill(bits)[::-1], 2) for j in range(count)] if bits else [0]


def split_kernel(amps, mine, theirs, sem):
    core = lax.axis_index("row") % CORES
    copies = [
        pltpu.make_async_copy(amps.at[:, :, core], mine, sem.at[0]),
        pltpu.make_async_copy(amps.at[:, :, 1 - core], theirs, sem.at[1]),
    ]
    for copy in copies:
        copy.start()
    for copy in copies:
        copy.wait()


def split(amps):
    shape = jax.ShapeDtypeStruct(amps.shape[:2] + amps.shape[3:], amps.dtype)
    return pl.pallas_call(
        split_kernel,
        out_shape=[shape, shape],
        in_specs=[ANY],
        out_specs=[ANY, ANY],
        scratch_shapes=[pltpu.SemaphoreType.DMA((2,))],
        compiler_params=params(),
        name="split_rows",
    )(amps)


def select_kernel(per_source, away, flips, wanted, *rest):
    groups, outs, sem = rest[:CORES], rest[CORES:-1], rest[-1]
    me, row = lax.axis_index("col"), lax.axis_index("row")
    length = wanted.shape[2]
    source = me ^ away
    copies = []
    for n, flip in enumerate(flips):
        other = me ^ flip
        for g in range(CORES):
            first = second = count = jnp.int32(0)
            for k in range(length):
                w = wanted[other, row ^ g, k]
                mine = w // per_source == source
                tile = w % per_source
                first = jnp.where(mine & (count == 0), tile, first)
                second = jnp.where(mine & (count == 1), tile, second)
                count = count + mine.astype(jnp.int32)
            found = (first, second)
            for slot in range(CAP):
                start = pl.multiple_of(found[slot] * TILE, TILE)
                copy = pltpu.make_async_copy(groups[g].at[:, pl.ds(start, TILE)], outs[n].at[g, slot], sem.at[n, g, slot])
                copy.start()
                copies.append(copy)
    for copy in copies:
        copy.wait()


def select(wanted, groups, per_source, away, flips):
    rows = groups[0].shape[0]
    shape = jax.ShapeDtypeStruct((CORES, CAP, rows, TILE), groups[0].dtype)
    return pl.pallas_call(
        functools.partial(select_kernel, per_source, away, flips),
        out_shape=[shape] * len(flips),
        in_specs=[VMEM] + [ANY] * CORES,
        out_specs=[ANY] * len(flips),
        scratch_shapes=[pltpu.SemaphoreType.DMA((len(flips), CORES, CAP))],
        compiler_params=params(),
        name="select_tiles",
    )(wanted, *groups)


def choice_kernel(per_source, away, flips, wanted, *outs):
    me, row = lax.axis_index("col"), lax.axis_index("row")
    length = wanted.shape[2]
    source = me ^ away
    one = (lax.broadcasted_iota(jnp.int32, (TILE, TILE), 0) == lax.broadcasted_iota(jnp.int32, (TILE, TILE), 1)).astype(outs[0].dtype)
    for g, out in enumerate(outs):
        out[...] = jnp.zeros_like(out)
        for n, flip in enumerate(flips):
            other = me ^ flip

            def step(k, count):
                w = wanted[other, row ^ g, k]
                mine = w // per_source == source
                at = pl.ds(pl.multiple_of((w % per_source) * TILE, TILE), TILE)
                for slot in range(CAP):

                    @pl.when(mine & (count == slot))
                    def _():
                        low = (n * CAP + slot) * TILE
                        out[at, low:low + TILE] = one

                return count + mine.astype(jnp.int32)

            lax.fori_loop(0, length, step, jnp.int32(0))


def choice(wanted, per_source, away, flips, dtype):
    shape = jax.ShapeDtypeStruct((per_source * TILE, len(flips) * CAP * TILE), dtype)
    return pl.pallas_call(
        functools.partial(choice_kernel, per_source, away, flips),
        out_shape=[shape] * CORES,
        in_specs=[SMEM],
        out_specs=[VMEM] * CORES,
        compiler_params=params(4 * shape.size * CORES),
        name="choice_matrices",
    )(wanted)


def pass_on_kernel(ranges, *refs):
    groups, choices, outs = refs[:CORES], refs[CORES:2 * CORES], refs[2 * CORES:]
    count = len(outs) // len(ranges)
    for g in range(CORES):
        x = jnp.dot(groups[g][...], choices[g][...], preferred_element_type=jnp.float32).astype(outs[0].dtype)
        for m, (start, stop) in enumerate(ranges):
            for n in range(count):
                for slot in range(CAP):
                    low = (n * CAP + slot) * TILE
                    outs[m * count + n][g, slot] = x[start:stop, low:low + TILE]


def pass_on(groups, choices, ranges):
    rows, chosen = groups[0].shape[0], choices[0].shape[1]
    shapes = [jax.ShapeDtypeStruct((CORES, CAP, stop - start, TILE), groups[0].dtype) for start, stop in ranges for _ in range(chosen // (CAP * TILE))]
    size = sum(2 * x.size for x in (*groups, *choices)) + 4 * CORES * rows * chosen * 2
    return pl.pallas_call(
        functools.partial(pass_on_kernel, ranges),
        out_shape=shapes,
        in_specs=[VMEM] * (2 * CORES),
        out_specs=[VMEM] * len(shapes),
        compiler_params=params(size),
        name="pass_on_tiles",
    )(*groups, *choices)


def arrange_kernel(per_source, top, wanted, *refs):
    blocks, (early, far) = refs[:CORES], refs[CORES:]
    me, row = lax.axis_index("col"), lax.axis_index("row")
    length = wanted.shape[2]
    for part in (early, far):
        part[...] = jnp.zeros_like(part)
    near_base = CORES * per_source
    whole_base = near_base + CORES * CAP * (top - 1)
    for g in range(CORES):

        def place(k, carry):
            w = wanted[me, row ^ g, k]
            source = w // per_source
            slot = lax.fori_loop(0, k, lambda i, n: n + (wanted[me, row ^ g, i] // per_source == source).astype(jnp.int32), jnp.int32(0))
            away, tile = source ^ me, w % per_source
            passed = CAP * (CORES * (lax.rem(away, top) - 1) + g) + slot
            rows = blocks[g][pl.ds(pl.multiple_of(k * TILE, TILE), TILE)]

            def put(part, condition, at):
                @pl.when(condition)
                def _():
                    part[pl.ds(pl.multiple_of(at * TILE, TILE), TILE)] = rows

            put(early, away == 0, g * per_source + tile)
            put(early, (away > 0) & (away < top), near_base + passed)
            put(early, away == top, whole_base + g * per_source + tile)
            put(far, away > top, passed)
            return carry

        lax.fori_loop(0, length, place, 0)


def arrange(wanted, blocks, per_source, top):
    depth, width = blocks[0].shape
    passed = CORES * CAP * (top - 1)
    depths = [TILE * n for n in (2 * CORES * per_source + passed, passed)]
    part = width if depth <= 1024 else width // 4
    size = 4 * part * (CORES * depth + sum(depths))
    return pl.pallas_call(
        functools.partial(arrange_kernel, per_source, top),
        grid=(width // part,),
        out_shape=[jax.ShapeDtypeStruct((n, width), blocks[0].dtype) for n in depths],
        in_specs=[SMEM] + [pl.BlockSpec((depth, part), lambda n: (0, n))] * CORES,
        out_specs=[pl.BlockSpec((n, part), lambda n: (0, n)) for n in depths],
        compiler_params=params(size),
        name="arrange_block",
    )(wanted, *blocks)


def code(x):
    most = jnp.max(jnp.abs(x), axis=1, keepdims=True)
    power = jnp.clip(jnp.ceil(jnp.log2(jnp.maximum(most, LEAST))), -125.0, 120.0)
    scaled = jnp.floor(x * jnp.exp2(-power) * STEPS + 0.5)
    scaled = jnp.clip(scaled, -32767.0, 32767.0).astype(jnp.int32).astype(jnp.int16)
    powers = jnp.broadcast_to(power, (x.shape[0], TILE)).astype(jnp.int32).astype(jnp.int16)
    return scaled, powers


def decode(coded):
    width = coded.shape[1] - TILE
    power = coded[:, width:].astype(jnp.int32).astype(jnp.float32)[:, :1]
    return coded[:, :width].astype(jnp.int32).astype(jnp.float32) * (1 / STEPS) * jnp.exp2(power)


def steps(rows):
    size = 64 if rows % 64 == 0 else 32 if rows % 32 == 0 else 16
    return [slice(start, start + size) for start in range(0, rows, size)]


def put_coded(out, at, x):
    width = x.shape[1]
    out[at, :width], out[at, width:] = code(x)


def fill(left, source, units, flip, depth, at):
    y = (lax.axis_index("row") // CORES) ^ flip
    span = units[1] - units[0]
    low = units[0] if source.shape[-4] > span else 0
    rows = pl.ds(at, span * source.shape[-2])
    if len(source.shape) == 4:
        tiles = [source[low:low + span, y]]
    else:
        tiles = [source[g, slot, low:low + span, y] for g in range(source.shape[0]) for slot in range(CAP)]
    for tile in tiles:
        width = tile.shape[-1]
        left[rows, depth:depth + width] = tile.reshape(-1, width)
        depth += width
    return depth


def contract_kernel(count, pieces, coded, places, *refs):
    sources, block = refs[:count], refs[count]
    before, outs, left = refs[count + 1:-1 - len(pieces)], refs[-1 - len(pieces):-1], refs[-1]
    base = 0
    for n, (units, flips) in enumerate(pieces):
        rows = outs[n].shape[0] // len(flips)
        for j, flip in enumerate(flips):
            depth = 0
            for source in sources:
                depth = fill(left, source, units, flip, depth, base + j * rows)
        base += outs[n].shape[0]
    product = jnp.dot(left[...], block[places[0]:places[1]], preferred_element_type=jnp.float32)
    base = 0
    for n in range(len(pieces)):
        rows = outs[n].shape[0]
        x = product[base:base + rows]
        base += rows
        if before:
            x = before[n][...] + x
        if coded:
            put_coded(outs[n], slice(None), x)
        else:
            outs[n][...] = x


def contract(sources, block, pieces, before=(), coded=False, places=None):
    places = places or (0, block.shape[0])
    depth, width = places[1] - places[0], block.shape[1]
    rows = [(units[1] - units[0]) * sources[0].shape[-2] * len(flips) for units, flips in pieces]
    if coded:
        shapes = [jax.ShapeDtypeStruct((n, width + TILE), jnp.int16) for n in rows]
    else:
        shapes = [jax.ShapeDtypeStruct((n, width), jnp.float32) for n in rows]
    size = 2 * (block.size + depth * sum(rows)) + 16 * width * sum(rows) + sum(2 * x.size for x in sources)
    return pl.pallas_call(
        functools.partial(contract_kernel, len(sources), pieces, coded, places),
        out_shape=shapes,
        in_specs=[VMEM] * (len(sources) + 1 + len(before)),
        out_specs=[VMEM] * len(shapes),
        scratch_shapes=[pltpu.VMEM((sum(rows), depth), block.dtype)],
        compiler_params=params(size),
        name="contract_tiles",
    )(*sources, block, *before)


def fold_kernel(keep, arrived, send, kept):
    half = kept.shape[0]
    for at in steps(half):
        put_coded(send, at, keep[at] + decode(arrived[at]))
    for at in steps(half):
        low = slice(at.start + half, at.stop + half)
        kept[at] = keep[low] + decode(arrived[low])


def fold(keep, arrived):
    half, width = keep.shape[0] // 2, keep.shape[1]
    return pl.pallas_call(
        fold_kernel,
        out_shape=[jax.ShapeDtypeStruct((half, width + TILE), jnp.int16), jax.ShapeDtypeStruct((half, width), jnp.float32)],
        in_specs=[VMEM, VMEM],
        out_specs=[VMEM, VMEM],
        compiler_params=params(),
        name="fold_rows",
    )(keep, arrived)


def finish_kernel(*refs):
    out, base = refs[-1], 0
    for keep, arrived in zip(refs[:-1:2], refs[1:-1:2]):
        for at in steps(keep.shape[0]):
            out[base + at.start:base + at.stop] = (keep[at] + decode(arrived[at])).astype(out.dtype)
        base += keep.shape[0]


def finish(pieces):
    flat = [x for piece in pieces for x in piece]
    rows = sum(keep.shape[0] for keep, _ in pieces)
    return pl.pallas_call(
        finish_kernel,
        out_shape=jax.ShapeDtypeStruct((rows, flat[0].shape[1]), jnp.bfloat16),
        in_specs=[VMEM] * len(flat),
        out_specs=VMEM,
        compiler_params=params(),
        name="finish_rows",
    )(*flat)


def reorder_kernel(tiles_held, owner, received, out):
    for t in range(owner.shape[1]):
        at = owner[0, t]
        start = pl.multiple_of((at % tiles_held) * TILE, TILE)
        out[:, t * TILE:(t + 1) * TILE] = received[at // tiles_held, :, pl.ds(start, TILE)]


def reorder(owner, received):
    columns, rows, width = received.shape
    return pl.pallas_call(
        functools.partial(reorder_kernel, width // TILE),
        out_shape=jax.ShapeDtypeStruct((rows, columns * width), received.dtype),
        in_specs=[VMEM, VMEM],
        out_specs=VMEM,
        compiler_params=params(),
        name="reorder_tiles",
    )(owner.reshape(1, -1), received)


def swap(x, axis, flip):
    return lax.ppermute(x, axis, [(i, i ^ flip) for i in range(lax.axis_size(axis))])


def body(amplitudes, integrals, wanted, owner):
    columns = lax.axis_size("col")
    parts = lax.axis_size("row")
    ys = parts // CORES
    pairs = amplitudes.shape[0]
    per_source = amplitudes.shape[1] // TILE
    per_device = pairs // (columns * parts)
    top = columns // 2
    low = list(range(1, top))
    b = max(per_device, 16)
    units = pairs // (parts * b)
    if b != per_device:
        amplitudes = amplitudes.reshape(units, columns // units, parts, per_device, -1).transpose(0, 2, 1, 3, 4)
    order = halving_order(ys)
    slots = [order[:ys // 2], order[ys // 2:]]
    first = units * FIRST // 4
    bounds = [(0, first), (first, units)] if first < units else [(0, units)]

    def whole(x):
        return x.reshape(units, ys, b, -1)

    def flat(x):
        return x.reshape(units * ys * b, -1)

    def spread(picked):
        return [swap(x, "col", f).reshape(CORES, CAP, -1, ys, b, TILE) for x, f in zip(picked, low)]

    mine, theirs = split(amplitudes.reshape(units, ys, CORES, b, -1))
    own = [mine, swap(theirs, "row", 1)]
    early = swap(mine, "col", top)
    picked = select(wanted, [flat(x) for x in own], per_source, 0, low)
    nearby = spread(picked)
    mirrors = [early, swap(own[1], "col", top)]
    blocks = arrange(wanted, [integrals, swap(integrals, "row", 1)], per_source, top)
    late_wanted, *blocks = lax.optimization_barrier((wanted, *blocks))
    choices = choice(late_wanted, per_source, top, low, amplitudes.dtype)
    *mirrors, early_block, far_block, choices, nearby[top // 2 - 1] = lax.optimization_barrier((*mirrors, *blocks, choices, nearby[top // 2 - 1]))
    mirrors = [whole(x) for x in mirrors]
    height = ys * b
    passed = pass_on([flat(x) for x in mirrors], choices, [(lo * height, hi * height) for lo, hi in bounds])
    groups = [passed[n:n + len(low)] for n in range(0, len(passed), len(low))]
    far = [spread(groups[0])]
    sums = contract(own + nearby + mirrors, early_block, [(at, flips) for at in bounds for flips in slots])
    for group in groups[1:]:
        far.append(spread(group))
    pieces = []
    for n, (lo, hi) in enumerate(bounds):
        span = (0, hi - lo)
        last = far_block.shape[0] - CORES * CAP * TILE
        so_far = contract(far[n][:-1], far_block, [(span, x) for x in slots], sums[2 * n:2 * n + 2], places=(0, last))
        ends = (last, far_block.shape[0])
        send, = contract(far[n][-1:], far_block, [(span, slots[0])], so_far[:1], coded=True, places=ends)
        keep, = contract(far[n][-1:], far_block, [(span, slots[1])], so_far[1:], places=ends)
        bit = CORES
        while True:
            arrived = swap(send, "row", bit)
            bit *= 2
            if bit == parts:
                break
            send, keep = fold(keep, arrived)
        pieces.append((keep, arrived))
    held = finish(pieces).reshape(columns, per_device, -1)
    exchanged = lax.all_to_all(held, "col", split_axis=0, concat_axis=0, tiled=True)
    return reorder(owner, exchanged)


def solution(mesh):
    in_specs = (P(None, ("col", "row")), P("row", "col"), P(), P())
    out_specs = P(("col", "row"), None)
    return jax.shard_map(body, mesh=mesh, in_specs=in_specs, out_specs=out_specs, check_vma=False)
```
